128 devices in a mesh: fib: 32 (over y, x, z_lo), xs: 4 (over z_hi, core).
Axes of the slice: x: 4, y: 4, z: 4 (z_hi: 2, z_lo: 2; z = z_hi * 2 + z_lo), core: 2. Of those that a mesh axis runs over, the one named last changes fastest.
Arguments:
- inverse_blocks: bfloat16 [32, 1536, 128, 128], P('fib', 'xs')
- constraint_rows: bfloat16 [96, 32, 196608], P(None, 'fib', 'xs'), may hold values from -6 to 6
- probe: bfloat16 [8192, 128], P(('fib', 'xs')), may hold values from -6 to 6
- face_offset: int32 [32, 4], P('fib', 'xs'), may hold values from 1 to 3
- primal_ids: int32 [32, 4, 96], P('fib', 'xs'), may hold values from 0 to 8191, as said below
- active_counts: int32 [32, 4], P('fib', 'xs'), may hold values from 48 to 96
Outputs:
- face_basis: bfloat16 [96, 32, 1536], P(None, 'fib', 'xs')
- coarse_apply: float32 [8192, 128], P(('fib', 'xs'))
The draws below stay inside these ranges and needn't reach their ends.
Inputs may be any that keep to these rules, and one draw needn't show every extreme that they name: `primal_ids`: column j of subdomain s (s = f * 4 + x) belongs to an owner subdomain (s + t) mod 128 with t one of 0, 1, -1, 2, -2, 3, -3 and 64, owner subdomain o owning ids o * 64 to (o + 1) * 64 - 1; at most 16 columns of one subdomain go to one owner, and exactly 16 to some owner in every subdomain.
All inputs are finite; a program needn't handle non-finite values.
Results may differ from the reference program's by a relative error of at most 0.0055.
Values may be sent and summed in bfloat16 or wider, within the bound.
A program may use at most 128 MiB of HBM per device.

```python
import math
import jax
import jax.numpy as jnp
from jax import lax

PRIMALS = 96
B = 128
NB = 384
P_DEV = 64
R = 128
CAP = 16
NEAR = 8
ROWS_DEV = 49152
NPRIMAL = 8192
N_FIB = 32
N_XS = 4
DEVICES = 128


def draw_inverse_blocks(key, part):
    key = jax.random.fold_in(key, 3)
    key_off, key_diag = jax.random.split(key)
    shape = (N_FIB, N_XS * NB, B, B)
    offdiag = jax.random.normal(key_off, shape, jnp.float32)
    diagonal = jax.random.uniform(key_diag, shape[:3], jnp.float32, 1.0, 2.0)
    identity = jnp.eye(B, dtype=jnp.float32)
    blocks = offdiag * (0.5 / math.sqrt(B)) * (1.0 - identity) + diagonal[..., None] * identity
    return blocks.astype(jnp.bfloat16)


def owner_shift(k, devices_n):
    if k == 0:
        return 0
    if k == 7:
        return devices_n // 2
    if k % 2 == 1:
        return (k + 1) // 2
    return -(k // 2)


def one_subdomain(key, subdomain):
    key_full, key_other, key_order, key_local = jax.random.split(key, 4)
    full_owner = jax.random.randint(key_full, (), 0, NEAR)
    others = jax.random.permutation(key_other, (NEAR - 1) * CAP)[:PRIMALS - CAP]
    other_slots = others + jnp.where(others >= full_owner * CAP, CAP, 0)
    full_slots = full_owner * CAP + jnp.arange(CAP, dtype=jnp.int32)
    slots = jnp.concatenate([full_slots, other_slots.astype(jnp.int32)])
    slots = jax.random.permutation(key_order, slots)
    shift_table = jnp.array([owner_shift(k, DEVICES) for k in range(NEAR)], dtype=jnp.int32)
    owner = (subdomain + shift_table[slots // CAP]) % DEVICES
    within = jax.random.randint(key_local, (PRIMALS,), 0, P_DEV)
    return (owner * P_DEV + within).astype(jnp.int32)


def draw_primal_ids(key, part):
    key = jax.random.fold_in(key, 5)
    keys = jax.random.split(key, DEVICES)
    table = jax.vmap(one_subdomain)(keys, jnp.arange(DEVICES, dtype=jnp.int32))
    return table.reshape(N_FIB, N_XS, PRIMALS)


def place_ends(result, rng, smallest, largest):
    index_at = [jax.random.randint(jax.random.fold_in(rng, axis), (), 0, length) for axis, length in enumerate(result.shape)]
    longest = result.shape.index(max(result.shape))
    beside = index_at[:longest] + [(index_at[longest] + 1) % result.shape[longest]] + index_at[longest + 1:]
    return result.at[tuple(index_at)].set(smallest).at[tuple(beside)].set(largest)


def shard_levels(key, dims, cuts, low, top_value):
    factor_of, own = 1.0, jax.random.fold_in(key, 6)
    for dim, shards_of in cuts:
        heights = jnp.exp(jax.random.uniform(jax.random.fold_in(own, dim), (shards_of,), jnp.float32, low / len(cuts), top_value / len(cuts)))
        factor_of = factor_of * jnp.repeat(heights, dims[dim] // shards_of).reshape([-1 if axis == dim else 1 for axis in range(len(dims))])
    return factor_of


def centred(key, shape, width, limit, shards=(), held_as=jnp.bfloat16):
    factor_of = shard_levels(key, shape, shards, -0.22, 0.18) if shards else 1.0
    values = jax.random.normal(key, shape, jnp.float32) * width * factor_of
    return jnp.minimum(jnp.maximum(values, -limit), limit).astype(held_as)


def setup_inputs(seed: int = 0) -> dict:
    key_list = jax.random.split(jax.random.key(seed), 7)
    inverse_blocks = draw_inverse_blocks(jax.random.fold_in(key_list[6], 71), 0)
    constraint_rows = centred(key_list[1], (PRIMALS, N_FIB, N_XS * ROWS_DEV), 1.0, 6.0, ((1, 32), (2, 4)))
    probe = centred(key_list[2], (NPRIMAL, R), 1.0, 6.0, ((0, 128),))
    face_offset = place_ends(jax.random.randint(key_list[3], (N_FIB, N_XS), 1, N_XS), jax.random.fold_in(key_list[3], 1), 1, N_XS - 1).astype(jnp.int32)
    primal_ids = draw_primal_ids(jax.random.fold_in(key_list[6], 71), 0)
    active_counts = place_ends(jax.random.randint(key_list[5], (N_FIB, N_XS), PRIMALS // 2, PRIMALS + 1), jax.random.fold_in(key_list[5], 1), PRIMALS // 2, PRIMALS).astype(jnp.int32)
    return {"inverse_blocks": inverse_blocks, "constraint_rows": constraint_rows, "probe": probe, "face_offset": face_offset, "primal_ids": primal_ids, "active_counts": active_counts}


def solve_slice(pair):
    inverse_slice, rows_slice = pair
    right_side = rows_slice.reshape(PRIMALS, N_XS * NB, B).astype(jnp.float32)
    basis = jnp.einsum('nab,jnb->jna', inverse_slice.astype(jnp.float32), right_side)
    return basis.reshape(PRIMALS, N_XS, NB * B).astype(jnp.bfloat16)


def coarse_slice(pair):
    averaged, rows_slice = pair
    rows_three = rows_slice.reshape(PRIMALS, N_XS, NB * B).astype(jnp.float32)
    coarse = jnp.einsum('jxr,kxr->xjk', averaged.astype(jnp.float32), rows_three)
    return coarse / (NB * B)


def reference(inverse_blocks, constraint_rows, probe, face_offset, primal_ids, active_counts):
    rows_fibre = jnp.moveaxis(constraint_rows, 1, 0)
    basis = lax.map(solve_slice, (inverse_blocks, rows_fibre))
    low_face = basis[..., :B].astype(jnp.float32)
    cross_face = basis[..., B:2 * B].astype(jnp.float32)
    high_face = basis[..., NB * B - B:].astype(jnp.float32)
    new_low = (0.5 * (low_face + jnp.roll(high_face, 1, axis=0))).astype(jnp.bfloat16)
    new_high = (0.5 * (high_face + jnp.roll(low_face, -1, axis=0))).astype(jnp.bfloat16)
    partner = (jnp.arange(N_XS, dtype=jnp.int32)[None, :] + face_offset) % N_XS
    partner_index = jnp.broadcast_to(partner[:, None, :, None], cross_face.shape)
    partner_face = jnp.take_along_axis(cross_face, partner_index, axis=2)
    new_cross = (0.5 * (cross_face + partner_face)).astype(jnp.bfloat16)
    faces = jnp.concatenate([new_low, new_cross, new_high], axis=-1)
    face_basis = jnp.transpose(faces, (1, 0, 2, 3)).reshape(PRIMALS, N_FIB, N_XS * 3 * B)
    averaged = jnp.concatenate([new_low, new_cross, basis[..., 2 * B:NB * B - B], new_high], axis=-1)
    coarse = lax.map(coarse_slice, (averaged, rows_fibre))
    columns = jnp.arange(PRIMALS, dtype=jnp.int32)
    active = (columns[None, None, :] < active_counts[..., None]).astype(jnp.float32)
    coarse = coarse * active[..., :, None] * active[..., None, :]
    probe_rows = jnp.take(probe, primal_ids, axis=0).astype(jnp.float32)
    partial_value = jnp.einsum('fxjk,fxkr->fxjr', coarse, probe_rows, precision=lax.Precision.HIGHEST)
    coarse_apply = jax.ops.segment_sum(partial_value.reshape(-1, R), primal_ids.reshape(-1), num_segments=P_DEV * DEVICES)
    return face_basis, coarse_apply
```

```python
import functools

import jax
import jax.numpy as jnp
from jax import lax
from jax.experimental import pallas as pl
from jax.experimental.pallas import tpu as pltpu
from jax.sharding import PartitionSpec as P

SHIFTS = (0, 1, -1, 2, -2, 3, -3, 64)
NEAR = 8
GREETED = (1, -1, 2, -2, 3, -3, 4, -4, 64)
CHUNK = 20
MESH = pl.DeviceIdType.MESH
NT = (((1,), (1,)), ((), ()))
NN = (((1,), (0,)), ((), ()))
TN = (((0,), (0,)), ((), ()))
BF = jnp.bfloat16
F32 = jnp.float32


def dot(a, b, dims):
    return lax.dot_general(a, b, dims, preferred_element_type=F32)


def kernel(
    n_fib,
    n_xs,
    inv_hbm,
    rows_hbm,
    probe_hbm,
    ids_ref,
    offset_ref,
    count_ref,
    face_out,
    apply_out,
    inv_v,
    rows_v,
    inv_e,
    rows_e,
    own_v,
    fib_v,
    cross_v,
    near_v,
    select_v,
    part_v,
    recv_v,
    local_sem,
    inv_sem,
    rows_sem,
    fib_send,
    fib_recv,
    cross_send,
    cross_recv,
    probe_send,
    probe_recv,
    part_send,
    part_recv,
):
    n_dev = n_fib * n_xs
    chunks = inv_v.shape[0]
    block = inv_v.shape[2]
    blocks = inv_hbm.shape[0]
    primals, rows_dev = rows_hbm.shape
    owned = probe_hbm.shape[0]
    f = lax.axis_index("fib")
    x = lax.axis_index("xs")
    me = f * n_xs + x

    def at(shift):
        index = lax.rem(me + (shift + n_dev), n_dev)
        return (lax.div(index, n_xs), lax.rem(index, n_xs))

    barrier = pltpu.get_barrier_semaphore()
    for shift in GREETED:
        pl.semaphore_signal(barrier, inc=1, device_id=at(shift), device_id_type=MESH)

    ends = [
        pltpu.make_async_copy(inv_hbm.at[pl.ds(0, 2)], inv_e.at[pl.ds(0, 2)], local_sem.at[0]),
        pltpu.make_async_copy(inv_hbm.at[pl.ds(blocks - 2, 2)], inv_e.at[pl.ds(2, 2)], local_sem.at[1]),
        pltpu.make_async_copy(rows_hbm.at[:, pl.ds(0, 2 * block)], rows_e.at[0], local_sem.at[2]),
        pltpu.make_async_copy(
            rows_hbm.at[:, pl.ds(rows_dev - 2 * block, 2 * block)], rows_e.at[1], local_sem.at[3]
        ),
    ]
    own_probe = pltpu.make_async_copy(probe_hbm, near_v.at[pl.ds(0, owned)], local_sem.at[4])
    for copy in ends:
        copy.start()
    own_probe.start()

    def chunk_copies(c):
        width = CHUNK * block
        return (
            pltpu.make_async_copy(inv_hbm.at[pl.ds(2 + c * CHUNK, CHUNK)], inv_v.at[c], inv_sem.at[c]),
            pltpu.make_async_copy(
                rows_hbm.at[:, pl.ds(pl.multiple_of(2 * block + c * width, block), width)],
                rows_v.at[c],
                rows_sem.at[c],
            ),
        )

    def start_chunk(c, carry):
        for copy in chunk_copies(c):
            copy.start()
        return carry

    lax.fori_loop(0, chunks, start_chunk, 0)

    ids = ids_ref[...]
    owner = lax.shift_right_logical(ids, 6)
    delta = owner - me
    delta = jnp.where(delta < 0, delta + n_dev, delta)
    slot = jnp.zeros_like(delta)
    for k in range(1, NEAR):
        slot = jnp.where(delta == (SHIFTS[k] % n_dev), k, slot)
    target = slot * owned + (ids - owner * owned)
    lane = lax.broadcasted_iota(jnp.int32, ids.shape, 1)
    target = jnp.where(lane < count_ref[0, 0], target, -1)
    wanted = lax.broadcasted_iota(jnp.int32, (NEAR * owned, primals), 0)
    select_v[...] = jnp.where(wanted == target, 1.0, 0.0).astype(BF)

    for copy in ends:
        copy.wait()

    def edge(e, h):
        return dot(rows_e[e, :, h * block : (h + 1) * block], inv_e[2 * e + h], NT).astype(BF)

    own_v[0] = edge(0, 0)
    own_v[1] = edge(0, 1)
    own_v[2] = edge(1, 1)
    inner = edge(1, 0)

    pl.semaphore_wait(barrier, len(GREETED))
    before = (lax.rem(f + n_fib - 1, n_fib), x)
    after = (lax.rem(f + 1, n_fib), x)

    def remote(src, dst, send, recv, device):
        return pltpu.make_async_remote_copy(
            src_ref=src, dst_ref=dst, send_sem=send, recv_sem=recv, device_id=device, device_id_type=MESH
        )

    sends = [
        remote(own_v.at[2], fib_v.at[0], fib_send.at[0], fib_recv.at[0], after),
        remote(own_v.at[0], fib_v.at[1], fib_send.at[1], fib_recv.at[1], before),
    ]
    for d in range(1, n_xs):
        to = (f, lax.rem(x + n_xs - d, n_xs))
        sends.append(remote(own_v.at[1], cross_v.at[d - 1], cross_send.at[d - 1], cross_recv.at[d - 1], to))
    for k in range(1, NEAR):
        sends.append(
            remote(
                probe_hbm,
                near_v.at[pl.ds(k * owned, owned)],
                probe_send.at[k - 1],
                probe_recv.at[k - 1],
                at(-SHIFTS[k]),
            )
        )
    for copy in sends:
        copy.start()

    def body(c, acc):
        for copy in chunk_copies(c):
            copy.wait()
        parts = []
        for i in range(CHUNK):
            parts.append(dot(rows_v[c, :, i * block : (i + 1) * block], inv_v[c, i], NT).astype(BF))
        return acc + dot(jnp.concatenate(parts, axis=1), rows_v[c], NT)

    coarse = lax.fori_loop(0, chunks, body, jnp.zeros((primals, primals), F32))

    own_probe.wait()
    for copy in sends:
        copy.wait()
    picked = dot(select_v[...], near_v[...], TN).astype(BF)

    offset = offset_ref[0, 0]
    partner = cross_v[0].astype(F32)
    for d in range(2, n_xs):
        partner = jnp.where(offset == d, cross_v[d - 1].astype(F32), partner)
    new_low = (0.5 * (own_v[0].astype(F32) + fib_v[0].astype(F32))).astype(BF)
    new_high = (0.5 * (own_v[2].astype(F32) + fib_v[1].astype(F32))).astype(BF)
    new_cross = (0.5 * (own_v[1].astype(F32) + partner)).astype(BF)
    face_out[:, 0:block] = new_low
    face_out[:, block : 2 * block] = new_cross
    face_out[:, 2 * block : 3 * block] = new_high
    coarse = coarse + dot(jnp.concatenate([new_low, new_cross], axis=1), rows_e[0], NT)
    coarse = coarse + dot(jnp.concatenate([inner, new_high], axis=1), rows_e[1], NT)
    coarse = coarse * (1.0 / rows_dev)

    def pieces(value):
        high = value.astype(BF)
        low = (value - high.astype(F32)).astype(BF)
        return high, low

    c_high, c_low = pieces(coarse)
    partial = dot(c_high, picked, NN) + dot(c_low, picked, NN)
    p_high, p_low = pieces(partial)
    dense = dot(select_v[...], p_high, NN) + dot(select_v[...], p_low, NN)
    part_v[...] = dense

    outs = []
    for k in range(1, NEAR):
        outs.append(
            remote(
                part_v.at[pl.ds(k * owned, owned)],
                recv_v.at[k - 1],
                part_send.at[k - 1],
                part_recv.at[k - 1],
                at(SHIFTS[k]),
            )
        )
    for copy in outs:
        copy.start()
    for copy in outs:
        copy.wait()
    total = part_v[0:owned, :]
    for k in range(1, NEAR):
        total = total + recv_v[k - 1]
    apply_out[...] = total


def shards(n_fib, n_xs, inverse_blocks, constraint_rows, probe, face_offset, primal_ids, active_counts):
    inv = inverse_blocks[0]
    rows = constraint_rows[:, 0, :]
    blocks, block, _ = inv.shape
    primals, rows_dev = rows.shape
    owned, vectors = probe.shape
    chunks = (blocks - 4) // CHUNK
    dma = pltpu.SemaphoreType.DMA
    faces, applied = pl.pallas_call(
        functools.partial(kernel, n_fib, n_xs),
        out_shape=(
            jax.ShapeDtypeStruct((primals, 3 * block), BF),
            jax.ShapeDtypeStruct((owned, vectors), F32),
        ),
        in_specs=[
            pl.BlockSpec(memory_space=pl.ANY),
            pl.BlockSpec(memory_space=pl.ANY),
            pl.BlockSpec(memory_space=pl.ANY),
            pl.BlockSpec(memory_space=pltpu.VMEM),
            pl.BlockSpec(memory_space=pltpu.SMEM),
            pl.BlockSpec(memory_space=pltpu.SMEM),
        ],
        out_specs=(
            pl.BlockSpec(memory_space=pltpu.VMEM),
            pl.BlockSpec(memory_space=pltpu.VMEM),
        ),
        scratch_shapes=[
            pltpu.VMEM((chunks, CHUNK, block, block), BF),
            pltpu.VMEM((chunks, primals, CHUNK * block), BF),
            pltpu.VMEM((4, block, block), BF),
            pltpu.VMEM((2, primals, 2 * block), BF),
            pltpu.VMEM((3, primals, block), BF),
            pltpu.VMEM((2, primals, block), BF),
            pltpu.VMEM((n_xs - 1, primals, block), BF),
            pltpu.VMEM((NEAR * owned, vectors), BF),
            pltpu.VMEM((NEAR * owned, primals), BF),
            pltpu.VMEM((NEAR * owned, vectors), F32),
            pltpu.VMEM((NEAR - 1, owned, vectors), F32),
            dma((5,)),
            dma((chunks,)),
            dma((chunks,)),
            dma((2,)),
            dma((2,)),
            dma((n_xs - 1,)),
            dma((n_xs - 1,)),
            dma((NEAR - 1,)),
            dma((NEAR - 1,)),
            dma((NEAR - 1,)),
            dma((NEAR - 1,)),
        ],
        compiler_params=pltpu.CompilerParams(
            collective_id=0, has_side_effects=True, vmem_limit_bytes=48 * 1024 * 1024
        ),
        name="coarse_setup",
    )(inv, rows, probe, primal_ids[0], face_offset, active_counts)
    return faces[:, None, :], applied


def solution(mesh):
    return jax.shard_map(
        functools.partial(shards, mesh.shape["fib"], mesh.shape["xs"]),
        mesh=mesh,
        in_specs=(
            P("fib", "xs", None, None),
            P(None, "fib", "xs"),
            P(("fib", "xs"), None),
            P("fib", "xs"),
            P("fib", "xs", None),
            P("fib", "xs"),
        ),
        out_specs=(P(None, "fib", "xs"), P(("fib", "xs"), None)),
        check_vma=False,
    )
```

```python
import functools

import jax
import jax.numpy as jnp
from jax import lax
from jax.experimental import pallas as pl
from jax.experimental.pallas import tpu as pltpu
from jax.sharding import PartitionSpec as P

SHIFTS = (0, 1, -1, 2, -2, 3, -3, 64)
NEAR = 8
GREETED = (1, -1, 2, -2, 3, -3, 4, -4, 64)
CHUNK = 38
CAP = 16
MIDDLE = 1
DEPTH = 4
MESH = pl.DeviceIdType.MESH
NT = (((1,), (1,)), ((), ()))
NN = (((1,), (0,)), ((), ()))
TN = (((0,), (0,)), ((), ()))
BF = jnp.bfloat16
F32 = jnp.float32


def dot(a, b, dims):
    return lax.dot_general(a, b, dims, preferred_element_type=F32)


def kernel(
    n_fib,
    n_xs,
    inv_hbm,
    rows_hbm,
    probe_hbm,
    ids_hbm,
    offset_hbm,
    count_hbm,
    face_out,
    apply_out,
    inv_v,
    rows_v,
    turned_a,
    turned_b,
    inv_e,
    rows_e,
    own_v,
    fib_v,
    cross_v,
    near_v,
    select_v,
    pack_v,
    where_v,
    places_v,
    part_v,
    recv_v,
    ids_v,
    offset_s,
    count_s,
    local_sem,
    inv_sem,
    rows_sem,
    fib_send,
    fib_recv,
    cross_send,
    cross_recv,
    probe_send,
    probe_recv,
    place_send,
    place_recv,
    part_send,
    part_recv,
):
    n_dev = n_fib * n_xs
    chunks = inv_v.shape[0]
    block = inv_v.shape[2]
    blocks = inv_hbm.shape[0]
    primals, rows_dev = rows_hbm.shape
    owned = probe_hbm.shape[0]
    f = lax.axis_index("fib")
    x = lax.axis_index("xs")
    me = f * n_xs + x

    def at(shift):
        index = lax.rem(me + (shift + n_dev), n_dev)
        return (lax.div(index, n_xs), lax.rem(index, n_xs))

    barrier = pltpu.get_barrier_semaphore()
    for shift in GREETED:
        pl.semaphore_signal(barrier, inc=1, device_id=at(shift), device_id_type=MESH)

    ends = [
        pltpu.make_async_copy(inv_hbm.at[pl.ds(0, 2)], inv_e.at[pl.ds(0, 2)], local_sem.at[0]),
        pltpu.make_async_copy(inv_hbm.at[pl.ds(blocks - 2, 2)], inv_e.at[pl.ds(2, 2)], local_sem.at[1]),
        pltpu.make_async_copy(rows_hbm.at[:, pl.ds(0, 2 * block)], rows_e.at[0], local_sem.at[2]),
        pltpu.make_async_copy(
            rows_hbm.at[:, pl.ds(rows_dev - 2 * block, 2 * block)], rows_e.at[1], local_sem.at[3]
        ),
    ]
    small = [
        pltpu.make_async_copy(ids_hbm, ids_v, local_sem.at[4]),
        pltpu.make_async_copy(offset_hbm, offset_s, local_sem.at[5]),
        pltpu.make_async_copy(count_hbm, count_s, local_sem.at[6]),
    ]
    own_probe = pltpu.make_async_copy(probe_hbm, near_v.at[pl.ds(0, owned)], local_sem.at[7])
    for copy in ends + small + [own_probe]:
        copy.start()

    width = CHUNK * block

    def inv_copy(c):
        return pltpu.make_async_copy(inv_hbm.at[pl.ds(2 + c * CHUNK, CHUNK)], inv_v.at[c], inv_sem.at[c])

    def rows_copy(c):
        start = pl.multiple_of(2 * block + c * width, block)
        return pltpu.make_async_copy(rows_hbm.at[:, pl.ds(start, width)], rows_v.at[c], rows_sem.at[c])

    def start_chunk(c, carry):
        rows_copy(c).start()
        inv_copy(c).start()
        return carry

    lax.fori_loop(0, DEPTH, start_chunk, 0)

    for copy in small:
        copy.wait()
    ids = ids_v[...]
    owner = lax.shift_right_logical(ids, 6)
    delta = owner - me
    delta = jnp.where(delta < 0, delta + n_dev, delta)
    slot = jnp.zeros_like(delta)
    for k in range(1, NEAR):
        slot = jnp.where(delta == (SHIFTS[k] % n_dev), k, slot)
    within = ids - owner * owned
    active = lax.broadcasted_iota(jnp.int32, ids.shape, 1) < count_s[0, 0]
    slot = jnp.where(active, slot, -1)
    wanted = lax.broadcasted_iota(jnp.int32, (NEAR * owned, primals), 0)
    select_v[...] = jnp.where(wanted == jnp.where(active, slot * owned + within, -1), 1.0, 0.0).astype(BF)
    member = lax.broadcasted_iota(jnp.int32, (2 * NEAR, primals), 0) == slot
    ahead = lax.broadcasted_iota(jnp.int32, (primals, primals), 0) < lax.broadcasted_iota(
        jnp.int32, (primals, primals), 1
    )
    counts = dot(jnp.where(member, 1.0, 0.0).astype(BF), jnp.where(ahead, 1.0, 0.0).astype(BF), NN)
    rank = jnp.sum(jnp.where(member, counts, 0.0), axis=0, keepdims=True).astype(jnp.int32)
    place = jnp.where(active, slot * CAP + rank, -1)
    pack = jnp.where(lax.broadcasted_iota(jnp.int32, (NEAR * CAP, primals), 0) == place, 1.0, 0.0).astype(BF)
    pack_v[...] = pack
    within_rows = jnp.broadcast_to(within.astype(F32), (2 * NEAR, primals)).astype(BF)
    where_v[...] = dot(within_rows, pack, NT).astype(BF)

    for copy in ends:
        copy.wait()

    def edge(e, h):
        return dot(rows_e[e, :, h * block : (h + 1) * block], inv_e[2 * e + h], NT).astype(BF)

    own_v[0] = edge(0, 0)
    own_v[1] = edge(0, 1)
    own_v[2] = edge(1, 1)
    inner = edge(1, 0)

    before = (lax.rem(f + n_fib - 1, n_fib), x)
    after = (lax.rem(f + 1, n_fib), x)

    def remote(src, dst, send, recv, device):
        return pltpu.make_async_remote_copy(
            src_ref=src, dst_ref=dst, send_sem=send, recv_sem=recv, device_id=device, device_id_type=MESH
        )

    sends = [
        remote(own_v.at[2], fib_v.at[0], fib_send.at[0], fib_recv.at[0], after),
        remote(own_v.at[0], fib_v.at[1], fib_send.at[1], fib_recv.at[1], before),
    ]
    for d in range(1, n_xs):
        to = (f, lax.rem(x + n_xs - d, n_xs))
        sends.append(remote(own_v.at[1], cross_v.at[d - 1], cross_send.at[d - 1], cross_recv.at[d - 1], to))
    for k in range(1, NEAR):
        sends.append(
            remote(
                probe_hbm,
                near_v.at[pl.ds(k * owned, owned)],
                probe_send.at[k - 1],
                probe_recv.at[k - 1],
                at(-SHIFTS[k]),
            )
        )
        sends.append(
            remote(where_v, places_v.at[k - 1], place_send.at[k - 1], place_recv.at[k - 1], at(SHIFTS[k]))
        )

    def turn(c, turned):
        for i in range(CHUNK):
            turned[i] = rows_v[c, :, i * block : (i + 1) * block].T

    def step(c, turned, acc):
        parts = [dot(inv_v[c, i], turned[i], NN).astype(BF) for i in range(CHUNK)]
        return acc + dot(rows_v[c], jnp.concatenate(parts, axis=0), NN)

    def body(p, acc):
        @pl.when(p == MIDDLE)
        def _():
            pl.semaphore_wait(barrier, len(GREETED))
            for copy in sends:
                copy.start()

        c = 2 * p

        @pl.when(c + DEPTH < chunks)
        def _():
            start_chunk(c + DEPTH, 0)
            start_chunk(c + DEPTH + 1, 0)

        rows_copy(c + 1).wait()
        inv_copy(c).wait()
        turn(c + 1, turned_b)
        acc = step(c, turned_a, acc)
        rows_copy(c + 2).wait()
        inv_copy(c + 1).wait()
        turn(c + 2, turned_a)
        return step(c + 1, turned_b, acc)

    rows_copy(0).wait()
    turn(0, turned_a)
    coarse = lax.fori_loop(0, chunks // 2 - 1, body, jnp.zeros((primals, primals), F32))

    rows_copy(chunks - 1).wait()
    inv_copy(chunks - 2).wait()
    inv_copy(chunks - 1).wait()
    turn(chunks - 1, turned_b)
    coarse = step(chunks - 2, turned_a, coarse)
    coarse = step(chunks - 1, turned_b, coarse)
    for copy in sends:
        copy.wait_recv()
    own_probe.wait()

    offset = offset_s[0, 0]
    partner = cross_v[0].astype(F32)
    for d in range(2, n_xs):
        partner = jnp.where(offset == d, cross_v[d - 1].astype(F32), partner)
    new_low = (0.5 * (own_v[0].astype(F32) + fib_v[0].astype(F32))).astype(BF)
    new_high = (0.5 * (own_v[2].astype(F32) + fib_v[1].astype(F32))).astype(BF)
    new_cross = (0.5 * (own_v[1].astype(F32) + partner)).astype(BF)
    face_out[:, 0:block] = new_low
    face_out[:, block : 2 * block] = new_cross
    face_out[:, 2 * block : 3 * block] = new_high
    coarse = coarse + dot(rows_e[0], jnp.concatenate([new_low, new_cross], axis=1), NT)
    coarse = coarse + dot(rows_e[1], jnp.concatenate([inner, new_high], axis=1), NT)
    picked = dot(near_v[...], select_v[...], TN).astype(BF)
    group = lax.broadcasted_iota(jnp.int32, (1, NEAR * CAP), 1) // CAP
    places = where_v[0:1, :].astype(F32)
    for k in range(1, NEAR):
        places = jnp.where(group == k, places_v[k - 1, 0:1, :].astype(F32), places)
    spread = lax.broadcasted_iota(jnp.int32, (owned, NEAR * CAP), 0) == places.astype(jnp.int32)
    spread = jnp.where(spread, 1.0, 0.0).astype(BF)

    coarse = coarse * (1.0 / rows_dev)

    def pieces(value):
        high = value.astype(BF)
        low = (value - high.astype(F32)).astype(BF)
        return high, low

    c_high, c_low = pieces(coarse)
    partial = dot(picked, c_high, NN) + dot(picked, c_low, NN)
    p_high, p_low = pieces(partial)

    outs = []
    for k in (7, 5, 6, 3, 4, 1, 2):
        rows_k = pl.ds(k * CAP, CAP)
        outs.append(remote(part_v.at[rows_k], recv_v.at[rows_k], part_send.at[k - 1], part_recv.at[k - 1], at(SHIFTS[k])))
    packed = dot(pack_v[...], p_high, NT) + dot(pack_v[...], p_low, NT)
    part_v[...] = packed
    for copy in outs:
        copy.start()
    recv_v[0:CAP] = packed[0:CAP]
    for copy in sends:
        copy.wait_send()
    for copy in outs:
        copy.wait_recv()
    r_high, r_low = pieces(recv_v[...])
    apply_out[...] = dot(spread, r_high, NN) + dot(spread, r_low, NN)
    for copy in outs:
        copy.wait_send()


def settle(faces_in, applied_in, faces_out, applied_out):
    faces_out[...] = faces_in[...]
    applied_out[...] = applied_in[...]


def shards(n_fib, n_xs, inverse_blocks, constraint_rows, probe, face_offset, primal_ids, active_counts):
    inv = inverse_blocks[0]
    rows = constraint_rows[:, 0, :]
    blocks, block, _ = inv.shape
    primals, rows_dev = rows.shape
    owned, vectors = probe.shape
    chunks = (blocks - 4) // CHUNK
    dma = pltpu.SemaphoreType.DMA
    faces, applied = pl.pallas_call(
        functools.partial(kernel, n_fib, n_xs),
        out_shape=(
            jax.ShapeDtypeStruct((primals, 3 * block), BF),
            jax.ShapeDtypeStruct((owned, vectors), F32),
        ),
        in_specs=[
            pl.BlockSpec(memory_space=pl.ANY),
            pl.BlockSpec(memory_space=pl.ANY),
            pl.BlockSpec(memory_space=pl.ANY),
            pl.BlockSpec(memory_space=pl.ANY),
            pl.BlockSpec(memory_space=pl.ANY),
            pl.BlockSpec(memory_space=pl.ANY),
        ],
        out_specs=(
            pl.BlockSpec(memory_space=pltpu.VMEM),
            pl.BlockSpec(memory_space=pltpu.VMEM),
        ),
        scratch_shapes=[
            pltpu.VMEM((chunks, CHUNK, block, block), BF),
            pltpu.VMEM((chunks, primals, CHUNK * block), BF),
            pltpu.VMEM((CHUNK, block, primals), BF),
            pltpu.VMEM((CHUNK, block, primals), BF),
            pltpu.VMEM((4, block, block), BF),
            pltpu.VMEM((2, primals, 2 * block), BF),
            pltpu.VMEM((3, primals, block), BF),
            pltpu.VMEM((2, primals, block), BF),
            pltpu.VMEM((n_xs - 1, primals, block), BF),
            pltpu.VMEM((NEAR * owned, vectors), BF),
            pltpu.VMEM((NEAR * owned, primals), BF),
            pltpu.VMEM((NEAR * CAP, primals), BF),
            pltpu.VMEM((2 * NEAR, NEAR * CAP), BF),
            pltpu.VMEM((NEAR - 1, 2 * NEAR, NEAR * CAP), BF),
            pltpu.VMEM((NEAR * CAP, vectors), F32),
            pltpu.VMEM((NEAR * CAP, vectors), F32),
            pltpu.VMEM((1, primals), jnp.int32),
            pltpu.SMEM((1, 1), jnp.int32),
            pltpu.SMEM((1, 1), jnp.int32),
            dma((8,)),
            dma((chunks,)),
            dma((chunks,)),
            dma((2,)),
            dma((2,)),
            dma((n_xs - 1,)),
            dma((n_xs - 1,)),
            dma((NEAR - 1,)),
            dma((NEAR - 1,)),
            dma((NEAR - 1,)),
            dma((NEAR - 1,)),
            dma((NEAR - 1,)),
            dma((NEAR - 1,)),
        ],
        compiler_params=pltpu.CompilerParams(
            collective_id=0, has_side_effects=True, vmem_limit_bytes=54 * 1024 * 1024
        ),
        name="coarse_setup",
    )(inv, rows, probe, primal_ids[0], face_offset, active_counts)
    faces, applied = pl.pallas_call(
        settle,
        out_shape=(
            jax.ShapeDtypeStruct((primals, 3 * block), BF),
            jax.ShapeDtypeStruct((owned, vectors), F32),
        ),
        in_specs=[pl.BlockSpec(memory_space=pltpu.VMEM)] * 2,
        out_specs=(pl.BlockSpec(memory_space=pltpu.VMEM), pl.BlockSpec(memory_space=pltpu.VMEM)),
        name="settle",
    )(faces, applied)
    return faces[:, None, :], applied


def solution(mesh):
    return jax.shard_map(
        functools.partial(shards, mesh.shape["fib"], mesh.shape["xs"]),
        mesh=mesh,
        in_specs=(
            P("fib", "xs", None, None),
            P(None, "fib", "xs"),
            P(("fib", "xs"), None),
            P("fib", "xs"),
            P("fib", "xs", None),
            P("fib", "xs"),
        ),
        out_specs=(P(None, "fib", "xs"), P(("fib", "xs"), None)),
        check_vma=False,
    )
```

```python
import functools

import jax
import jax.numpy as jnp
from jax import lax
from jax.experimental import pallas as pl
from jax.experimental.pallas import tpu as pltpu
from jax.sharding import PartitionSpec as P

SHIFTS = (0, 1, -1, 2, -2, 3, -3, 64)
NEAR = 8
GREETED = (1, -1, 2, -2, 3, -3, 4, -4, 64)
CHUNK = 38
CAP = 16
MIDDLE = 1
DEPTH = 4
MESH = pl.DeviceIdType.MESH
NT = (((1,), (1,)), ((), ()))
NN = (((1,), (0,)), ((), ()))
TN = (((0,), (0,)), ((), ()))
BF = jnp.bfloat16
F32 = jnp.float32


def dot(a, b, dims):
    return lax.dot_general(a, b, dims, preferred_element_type=F32)


def kernel(
    n_fib,
    n_xs,
    inv_hbm,
    rows_hbm,
    probe_hbm,
    ids_hbm,
    offset_hbm,
    count_hbm,
    face_out,
    apply_out,
    inv_v,
    rows_v,
    turned_a,
    turned_b,
    inv_e,
    rows_e,
    own_v,
    fib_v,
    cross_v,
    near_v,
    select_v,
    pack_v,
    where_v,
    places_v,
    part_v,
    recv_v,
    ids_v,
    offset_s,
    count_s,
    local_sem,
    inv_sem,
    rows_sem,
    fib_send,
    fib_recv,
    cross_send,
    cross_recv,
    probe_send,
    probe_recv,
    place_send,
    place_recv,
    part_send,
    part_recv,
):
    n_dev = n_fib * n_xs
    chunks = inv_v.shape[0]
    block = inv_v.shape[2]
    blocks = inv_hbm.shape[0]
    primals, rows_dev = rows_hbm.shape
    owned = probe_hbm.shape[0]
    f = lax.axis_index("fib")
    x = lax.axis_index("xs")
    me = f * n_xs + x

    def at(shift):
        index = lax.rem(me + (shift + n_dev), n_dev)
        return (lax.div(index, n_xs), lax.rem(index, n_xs))

    barrier = pltpu.get_barrier_semaphore()
    for shift in GREETED:
        pl.semaphore_signal(barrier, inc=1, device_id=at(shift), device_id_type=MESH)

    ends = [
        pltpu.make_async_copy(inv_hbm.at[pl.ds(0, 2)], inv_e.at[pl.ds(0, 2)], local_sem.at[0]),
        pltpu.make_async_copy(inv_hbm.at[pl.ds(blocks - 2, 2)], inv_e.at[pl.ds(2, 2)], local_sem.at[1]),
        pltpu.make_async_copy(rows_hbm.at[:, pl.ds(0, 2 * block)], rows_e.at[0], local_sem.at[2]),
        pltpu.make_async_copy(
            rows_hbm.at[:, pl.ds(rows_dev - 2 * block, 2 * block)], rows_e.at[1], local_sem.at[3]
        ),
    ]
    small = [
        pltpu.make_async_copy(ids_hbm, ids_v, local_sem.at[4]),
        pltpu.make_async_copy(offset_hbm, offset_s, local_sem.at[5]),
        pltpu.make_async_copy(count_hbm, count_s, local_sem.at[6]),
    ]
    own_probe = pltpu.make_async_copy(probe_hbm, near_v.at[pl.ds(0, owned)], local_sem.at[7])
    for copy in small + ends:
        copy.start()

    width = CHUNK * block

    def inv_copy(c):
        return pltpu.make_async_copy(inv_hbm.at[pl.ds(2 + c * CHUNK, CHUNK)], inv_v.at[c], inv_sem.at[c])

    def rows_copy(c):
        start = pl.multiple_of(2 * block + c * width, block)
        return pltpu.make_async_copy(rows_hbm.at[:, pl.ds(start, width)], rows_v.at[c], rows_sem.at[c])

    def start_chunk(c, carry):
        rows_copy(c).start()
        inv_copy(c).start()
        return carry

    lax.fori_loop(0, DEPTH, start_chunk, 0)
    own_probe.start()

    for copy in small + ends:
        copy.wait()
    rows_copy(0).wait()
    ids = ids_v[...]
    owner = lax.shift_right_logical(ids, 6)
    delta = owner - me
    delta = jnp.where(delta < 0, delta + n_dev, delta)
    slot = jnp.zeros_like(delta)
    for k in range(1, NEAR):
        slot = jnp.where(delta == (SHIFTS[k] % n_dev), k, slot)
    within = ids - owner * owned
    active = lax.broadcasted_iota(jnp.int32, ids.shape, 1) < count_s[0, 0]
    slot = jnp.where(active, slot, -1)
    wanted = lax.broadcasted_iota(jnp.int32, (NEAR * owned, primals), 0)
    select_v[...] = jnp.where(wanted == jnp.where(active, slot * owned + within, -1), 1.0, 0.0).astype(BF)
    member = lax.broadcasted_iota(jnp.int32, (2 * NEAR, primals), 0) == slot
    ahead = lax.broadcasted_iota(jnp.int32, (primals, primals), 0) < lax.broadcasted_iota(
        jnp.int32, (primals, primals), 1
    )
    counts = dot(jnp.where(member, 1.0, 0.0).astype(BF), jnp.where(ahead, 1.0, 0.0).astype(BF), NN)
    rank = jnp.sum(jnp.where(member, counts, 0.0), axis=0, keepdims=True).astype(jnp.int32)
    place = jnp.where(active, slot * CAP + rank, -1)
    pack = jnp.where(lax.broadcasted_iota(jnp.int32, (NEAR * CAP, primals), 0) == place, 1.0, 0.0).astype(BF)
    pack_v[...] = pack
    within_rows = jnp.broadcast_to(within.astype(F32), (2 * NEAR, primals)).astype(BF)
    where_v[...] = dot(within_rows, pack, NT).astype(BF)

    def edge(e, h):
        return dot(rows_e[e, :, h * block : (h + 1) * block], inv_e[2 * e + h], NT).astype(BF)

    def turn(c, turned):
        for i in range(CHUNK):
            turned[i] = rows_v[c, :, i * block : (i + 1) * block].T

    turn(0, turned_a)
    own_v[0] = edge(0, 0)
    own_v[1] = edge(0, 1)
    own_v[2] = edge(1, 1)
    inner = edge(1, 0)

    before = (lax.rem(f + n_fib - 1, n_fib), x)
    after = (lax.rem(f + 1, n_fib), x)

    def remote(src, dst, send, recv, device):
        return pltpu.make_async_remote_copy(
            src_ref=src, dst_ref=dst, send_sem=send, recv_sem=recv, device_id=device, device_id_type=MESH
        )

    sends = [
        remote(own_v.at[2], fib_v.at[0], fib_send.at[0], fib_recv.at[0], after),
        remote(own_v.at[0], fib_v.at[1], fib_send.at[1], fib_recv.at[1], before),
    ]
    for d in range(1, n_xs):
        to = (f, lax.rem(x + n_xs - d, n_xs))
        sends.append(remote(own_v.at[1], cross_v.at[d - 1], cross_send.at[d - 1], cross_recv.at[d - 1], to))
    for k in range(1, NEAR):
        sends.append(
            remote(
                probe_hbm,
                near_v.at[pl.ds(k * owned, owned)],
                probe_send.at[k - 1],
                probe_recv.at[k - 1],
                at(-SHIFTS[k]),
            )
        )
        sends.append(
            remote(where_v, places_v.at[k - 1], place_send.at[k - 1], place_recv.at[k - 1], at(SHIFTS[k]))
        )

    def step(c, turned, acc):
        parts = [dot(inv_v[c, i], turned[i], NN).astype(BF) for i in range(CHUNK)]
        return acc + dot(rows_v[c], jnp.concatenate(parts, axis=0), NN)

    def body(p, acc):
        @pl.when(p == MIDDLE)
        def _():
            pl.semaphore_wait(barrier, len(GREETED))
            for copy in sends:
                copy.start()

        c = 2 * p

        @pl.when(c + DEPTH < chunks)
        def _():
            start_chunk(c + DEPTH, 0)
            start_chunk(c + DEPTH + 1, 0)

        rows_copy(c + 1).wait()
        inv_copy(c).wait()
        turn(c + 1, turned_b)
        acc = step(c, turned_a, acc)
        rows_copy(c + 2).wait()
        inv_copy(c + 1).wait()
        turn(c + 2, turned_a)
        return step(c + 1, turned_b, acc)

    coarse = lax.fori_loop(0, chunks // 2 - 1, body, jnp.zeros((primals, primals), F32))

    rows_copy(chunks - 1).wait()
    inv_copy(chunks - 2).wait()
    inv_copy(chunks - 1).wait()
    turn(chunks - 1, turned_b)
    coarse = step(chunks - 2, turned_a, coarse)
    coarse = step(chunks - 1, turned_b, coarse)
    for copy in sends:
        copy.wait_recv()
    own_probe.wait()

    offset = offset_s[0, 0]
    partner = cross_v[0].astype(F32)
    for d in range(2, n_xs):
        partner = jnp.where(offset == d, cross_v[d - 1].astype(F32), partner)
    new_low = (0.5 * (own_v[0].astype(F32) + fib_v[0].astype(F32))).astype(BF)
    new_high = (0.5 * (own_v[2].astype(F32) + fib_v[1].astype(F32))).astype(BF)
    new_cross = (0.5 * (own_v[1].astype(F32) + partner)).astype(BF)
    face_out[:, 0:block] = new_low
    face_out[:, block : 2 * block] = new_cross
    face_out[:, 2 * block : 3 * block] = new_high
    coarse = coarse + dot(rows_e[0], jnp.concatenate([new_low, new_cross], axis=1), NT)
    coarse = coarse + dot(rows_e[1], jnp.concatenate([inner, new_high], axis=1), NT)
    picked = dot(near_v[...], select_v[...], TN).astype(BF)
    group = lax.broadcasted_iota(jnp.int32, (1, NEAR * CAP), 1) // CAP
    places = where_v[0:1, :].astype(F32)
    for k in range(1, NEAR):
        places = jnp.where(group == k, places_v[k - 1, 0:1, :].astype(F32), places)
    spread = lax.broadcasted_iota(jnp.int32, (owned, NEAR * CAP), 0) == places.astype(jnp.int32)
    spread = jnp.where(spread, 1.0, 0.0).astype(BF)

    coarse = coarse * (1.0 / rows_dev)

    def pieces(value):
        high = value.astype(BF)
        low = (value - high.astype(F32)).astype(BF)
        return high, low

    c_high, c_low = pieces(coarse)
    partial = dot(picked, c_high, NN) + dot(picked, c_low, NN)
    p_high, p_low = pieces(partial)

    outs = []
    for k in (7, 5, 6, 3, 4, 1, 2):
        rows_k = pl.ds(k * CAP, CAP)
        outs.append(remote(part_v.at[rows_k], recv_v.at[rows_k], part_send.at[k - 1], part_recv.at[k - 1], at(SHIFTS[k])))
    packed = dot(pack_v[...], p_high, NT) + dot(pack_v[...], p_low, NT)
    part_v[...] = packed
    for copy in outs:
        copy.start()
    recv_v[0:CAP] = packed[0:CAP]
    for copy in sends:
        copy.wait_send()
    for copy in outs:
        copy.wait_recv()
    r_high, r_low = pieces(recv_v[...])
    apply_out[...] = dot(spread, r_high, NN) + dot(spread, r_low, NN)
    for copy in outs:
        copy.wait_send()


def shards(n_fib, n_xs, inverse_blocks, constraint_rows, probe, face_offset, primal_ids, active_counts):
    inv = inverse_blocks[0]
    rows = constraint_rows[:, 0, :]
    blocks, block, _ = inv.shape
    primals, rows_dev = rows.shape
    owned, vectors = probe.shape
    chunks = (blocks - 4) // CHUNK
    dma = pltpu.SemaphoreType.DMA
    faces, applied = pl.pallas_call(
        functools.partial(kernel, n_fib, n_xs),
        out_shape=(
            jax.ShapeDtypeStruct((primals, 3 * block), BF),
            jax.ShapeDtypeStruct((owned, vectors), F32),
        ),
        in_specs=[
            pl.BlockSpec(memory_space=pl.ANY),
            pl.BlockSpec(memory_space=pl.ANY),
            pl.BlockSpec(memory_space=pl.ANY),
            pl.BlockSpec(memory_space=pl.ANY),
            pl.BlockSpec(memory_space=pl.ANY),
            pl.BlockSpec(memory_space=pl.ANY),
        ],
        out_specs=(
            pl.BlockSpec(memory_space=pltpu.VMEM),
            pl.BlockSpec(memory_space=pltpu.VMEM),
        ),
        scratch_shapes=[
            pltpu.VMEM((chunks, CHUNK, block, block), BF),
            pltpu.VMEM((chunks, primals, CHUNK * block), BF),
            pltpu.VMEM((CHUNK, block, primals), BF),
            pltpu.VMEM((CHUNK, block, primals), BF),
            pltpu.VMEM((4, block, block), BF),
            pltpu.VMEM((2, primals, 2 * block), BF),
            pltpu.VMEM((3, primals, block), BF),
            pltpu.VMEM((2, primals, block), BF),
            pltpu.VMEM((n_xs - 1, primals, block), BF),
            pltpu.VMEM((NEAR * owned, vectors), BF),
            pltpu.VMEM((NEAR * owned, primals), BF),
            pltpu.VMEM((NEAR * CAP, primals), BF),
            pltpu.VMEM((2 * NEAR, NEAR * CAP), BF),
            pltpu.VMEM((NEAR - 1, 2 * NEAR, NEAR * CAP), BF),
            pltpu.VMEM((NEAR * CAP, vectors), F32),
            pltpu.VMEM((NEAR * CAP, vectors), F32),
            pltpu.VMEM((1, primals), jnp.int32),
            pltpu.SMEM((1, 1), jnp.int32),
            pltpu.SMEM((1, 1), jnp.int32),
            dma((8,)),
            dma((chunks,)),
            dma((chunks,)),
            dma((2,)),
            dma((2,)),
            dma((n_xs - 1,)),
            dma((n_xs - 1,)),
            dma((NEAR - 1,)),
            dma((NEAR - 1,)),
            dma((NEAR - 1,)),
            dma((NEAR - 1,)),
            dma((NEAR - 1,)),
            dma((NEAR - 1,)),
        ],
        compiler_params=pltpu.CompilerParams(
            collective_id=0, has_side_effects=True, vmem_limit_bytes=46 * 1024 * 1024
        ),
        name="coarse_setup",
    )(*(pltpu.with_memory_space_constraint(a, pltpu.HBM) for a in (inv, rows, probe, primal_ids[0])), face_offset, active_counts)
    return faces[:, None, :], applied


def solution(mesh):
    return jax.shard_map(
        functools.partial(shards, mesh.shape["fib"], mesh.shape["xs"]),
        mesh=mesh,
        in_specs=(
            P("fib", "xs", None, None),
            P(None, "fib", "xs"),
            P(("fib", "xs"), None),
            P("fib", "xs"),
            P("fib", "xs", None),
            P("fib", "xs"),
        ),
        out_specs=(P(None, "fib", "xs"), P(("fib", "xs"), None)),
        check_vma=False,
    )
```
